32 devices in a mesh: lon: 16 (over z, x, core), tp: 2 (over y).
Axes of the slice: x: 2, y: 2, z: 4, core: 2. Of those that a mesh axis runs over, the one named last changes fastest.
Arguments:
- image_tokens: bfloat16 [4096, 3072], P('lon', 'tp'), may hold values from -6 to 6
- style_tokens: bfloat16 [512, 3072], P('lon', 'tp'), may hold values from -6 to 6
- qkv_weight: bfloat16 [3, 3072, 2048], P(None, 'lon', 'tp'), may hold values from -0.109375 to 0.109375
- out_weight: bfloat16 [2048, 3072], P('tp', 'lon'), may hold values from -0.125 to 0.125
- query_gain: float32 [128], replicated, may hold values from 0.6 to 9, as said below
- key_gain: float32 [128], replicated, may hold values from 0.6 to 9, as said below
- attend_flags: int32 [16, 1], P('lon'), may hold values from 0 to 1
Outputs:
- mixed: bfloat16 [4096, 3072], P('lon', 'tp')
The draws below stay inside these ranges and needn't reach their ends.
Inputs may be any that keep to these rules, and one draw needn't show every extreme that they name: `query_gain`: positive gains. `key_gain`: positive gains.
All inputs are finite; a program needn't handle non-finite values.
Results may differ from the reference program's by a relative error of at most 0.015.
The reference program's roundings to bfloat16 on the way (of `weights` and `attended`) count: a program that leaves them out, or rounds other values in their place, can miss the bound.
Values may be sent and summed in bfloat16 or wider, within the bound.
A program may use at most 64 MiB of HBM per device.

```python
import math
import jax
import jax.numpy as jnp
from jax import lax

D = 3072
HEADS = 16
HEAD = 128
TOK_DEV = 256
HD = 2048
SLABS = 16
TOKENS = 4096
REF = 512


def draw_query_gain(key, part):
    inner = jax.random.fold_in(key, 11)
    return jax.random.uniform(inner, (HEAD,), jnp.float32, 0.6, 1.6)


def draw_key_gain(key, part):
    inner = jax.random.fold_in(key, 23)
    return jax.random.uniform(inner, (HEAD,), jnp.float32, 0.6, 1.6)


def set_ends(entries, stream_key, low, top_value):
    dims = entries.shape
    index_at = [jax.random.randint(jax.random.fold_in(stream_key, axis), (), 0, dims[axis]) for axis in range(len(dims))]
    entries = entries.at[tuple(index_at)].set(low)
    longest = dims.index(max(dims))
    index_at[longest] = (index_at[longest] + 1) % dims[longest]
    return entries.at[tuple(index_at)].set(top_value)


def level_of(key, extent, pieces, least, largest):
    factor_of = 1.0
    for axis_at, parts in pieces:
        heights = jax.random.uniform(jax.random.fold_in(jax.random.fold_in(key, 6), axis_at), (parts,), jnp.float32, least / len(pieces), largest / len(pieces))
        factor_of = factor_of * jnp.repeat(jnp.exp(heights), extent[axis_at] // parts).reshape((-1,) + (1,) * (len(extent) - 1 - axis_at))
    return factor_of


def gaussian(rng, extent, deviation, most, cuts=(), kind=jnp.bfloat16):
    drawn = deviation * jax.random.normal(rng, extent, jnp.float32)
    if cuts:
        drawn = drawn * level_of(rng, extent, cuts, -0.22, 0.18)
    return jnp.clip(drawn, -most, most).astype(kind)


def setup_inputs(seed: int = 0) -> dict:
    splits = jax.random.split(jax.random.key(seed), 8)
    return {
        "image_tokens": gaussian(splits[0], (TOKENS, D), 1.0, 6.0, ((0, 16), (1, 2))),
        "style_tokens": gaussian(splits[1], (REF, D), 1.0, 6.0, ((0, 16), (1, 2))),
        "qkv_weight": gaussian(splits[2], (3, D, HD), D ** -0.5, 0.109375, ((1, 16), (2, 2))),
        "out_weight": gaussian(splits[3], (HD, D), HD ** -0.5, 0.125, ((0, 2), (1, 16))),
        "query_gain": draw_query_gain(jax.random.fold_in(splits[7], 71), 0),
        "key_gain": draw_key_gain(jax.random.fold_in(splits[7], 71), 0),
        "attend_flags": set_ends(jax.random.randint(splits[6], (SLABS, 1), 0, 2), jax.random.fold_in(splits[6], 1), 0, 1).astype(jnp.int32),
    }


def head_norm(values, gain):
    return values * lax.rsqrt(lax.optimization_barrier(jnp.mean(values * values, axis=-1, keepdims=True)) + 1e-06) * gain

def reference(image_tokens, style_tokens, qkv_weight, out_weight, query_gain, key_gain, attend_flags):
    count = image_tokens.shape[0]
    slab_count = count // TOK_DEV
    ref_count = style_tokens.shape[0]
    proj = [jnp.dot(image_tokens, qkv_weight[j], preferred_element_type=jnp.float32) for j in range(3)]
    query = head_norm(proj[0].reshape(count, HEADS, HEAD), query_gain).astype(jnp.bfloat16)
    keys = head_norm(proj[1].reshape(count, HEADS, HEAD), key_gain).astype(jnp.bfloat16)
    values = proj[2].reshape(count, HEADS, HEAD).astype(jnp.bfloat16)
    ref_key = jnp.dot(style_tokens, qkv_weight[1], preferred_element_type=jnp.float32)
    ref_key = head_norm(ref_key.reshape(ref_count, HEADS, HEAD), key_gain).astype(jnp.bfloat16)
    ref_value = jnp.dot(style_tokens, qkv_weight[2], preferred_element_type=jnp.float32)
    ref_value = ref_value.reshape(ref_count, HEADS, HEAD).astype(jnp.bfloat16)
    query_slabs = query.reshape(slab_count, TOK_DEV, HEADS, HEAD)
    key_slabs = keys.reshape(slab_count, TOK_DEV, HEADS, HEAD)
    value_slabs = values.reshape(slab_count, TOK_DEV, HEADS, HEAD)

    def one_slab(packed):
        query_block, key_prev, key_own, key_next, value_prev, value_own, value_next, flags = packed
        key_set = jnp.concatenate([key_prev, key_own, key_next, ref_key], axis=0).astype(jnp.float32)
        value_set = jnp.concatenate([value_prev, value_own, value_next, ref_value], axis=0).astype(jnp.float32)
        scores = jnp.einsum('qhe,khe->hqk', query_block.astype(jnp.float32), key_set) / math.sqrt(HEAD)
        allowed = jnp.concatenate([jnp.ones((3 * TOK_DEV,), bool), jnp.full((ref_count,), flags[0] > 0)])
        scores = jnp.where(allowed[None, None, :], scores, -1e+30)
        peak = lax.optimization_barrier(jnp.max(scores, axis=-1, keepdims=True))
        expo = jnp.exp(scores - peak)
        weights = (expo / lax.optimization_barrier(jnp.sum(expo, axis=-1, keepdims=True))).astype(jnp.bfloat16)
        result = jnp.einsum('hqk,khe->qhe', weights.astype(jnp.float32), value_set)
        return result.astype(jnp.bfloat16).reshape(TOK_DEV, HEADS * HEAD)
    attended = lax.map(one_slab, (query_slabs, jnp.roll(key_slabs, 1, axis=0), key_slabs, jnp.roll(key_slabs, -1, axis=0), jnp.roll(value_slabs, 1, axis=0), value_slabs, jnp.roll(value_slabs, -1, axis=0), attend_flags))
    attended = attended.reshape(count, HEADS * HEAD)
    return jnp.dot(attended, out_weight, preferred_element_type=jnp.float32).astype(jnp.bfloat16)
```

```python
import functools
import math

import jax
import jax.numpy as jnp
from jax import lax
from jax.experimental import pallas as pl
from jax.experimental.pallas import tpu as pltpu
from jax.sharding import PartitionSpec as P

HEAD = 128
ITEMS = 5
MESH = pl.DeviceIdType.MESH
NT = (((1,), (1,)), ((), ()))


def normed(part, gain):
    return part * lax.rsqrt(jnp.mean(part * part, axis=-1, keepdims=True) + 1e-06) * gain


def kernel(
    n_lon,
    n_tp,
    image_ref,
    style_ref,
    qkv_ref,
    out_w_ref,
    query_gain_ref,
    key_gain_ref,
    flags_ref,
    mixed_ref,
    tokens,
    styles,
    weights,
    queries,
    keys,
    values,
    probs,
    attended,
    part,
    arrived,
    ring_send,
    ring_recv,
    sib_send,
    sib_recv,
    own_send,
    own_recv,
    tp_send,
    tp_recv,
    halo_send,
    halo_recv,
    fwd_send,
    fwd_recv,
    out_send,
    out_recv,
):
    count, feat = image_ref.shape
    style_rows = style_ref.shape[0]
    block = qkv_ref.shape[1]
    width = qkv_ref.shape[2]
    heads = width // HEAD
    key_count = keys.shape[0]
    outw = mixed_ref.shape[1]
    chips = n_lon // 2
    half_ring = chips // 2
    lon = lax.axis_index("lon")
    tp = lax.axis_index("tp")
    chip = lon // 2
    core = lon % 2
    odd = chip % 2
    place = (1 - odd) * (chip // 2) + odd * (chips - (chip + 1) // 2)

    def lon_at(position, side):
        position = lax.rem(position + 2 * chips, chips)
        upper = position // half_ring
        there = (1 - upper) * (2 * position) + upper * (2 * chips - 1 - 2 * position)
        return there * 2 + side

    right = {"lon": lon_at(place + 1, core)}
    left = {"lon": lon_at(place - 1, core)}
    sibling = {"lon": chip * 2 + 1 - core}
    after = {"lon": lax.rem(lon + 1, n_lon)}
    before = {"lon": lax.rem(lon + n_lon - 1, n_lon)}
    peers = [{"tp": lax.rem(tp + k, n_tp)} for k in range(1, n_tp)]

    low_w = block // 2 // 16 * 16
    low_s = style_rows // 2 // 16 * 16

    def slot(item, owner, half):
        if item == 0:
            total, low = style_rows, low_s
        else:
            total, low = block, low_w
        start, size = {0: (0, low), 1: (low, total - low), 2: (0, total)}[half]
        if item == 0:
            return styles.at[tp, owner % 2, owner // 2, pl.ds(start, size), :]
        return weights.at[item - 1, pl.ds(pl.multiple_of(owner * block, 16) + start, size), :]

    barrier = pltpu.get_barrier_semaphore()
    partners = [right, left, sibling, after, before] + peers
    for partner in partners:
        pl.semaphore_signal(barrier, inc=1, device_id=partner, device_id_type=MESH)

    styles[tp, core, chip] = style_ref[...]
    tokens[tp] = image_ref[...]
    own_rows = pl.ds(pl.multiple_of(lon * block, 16), block)
    for j in range(3):
        weights[j, own_rows, :] = qkv_ref[j]
    weights[3, own_rows, :] = out_w_ref[...]
    pl.semaphore_wait(barrier, len(partners))

    started = []

    def send(src, dst, send_sem, recv_sem, device):
        copy = pltpu.make_async_remote_copy(
            src_ref=src,
            dst_ref=dst,
            send_sem=send_sem,
            recv_sem=recv_sem,
            device_id=device,
            device_id_type=MESH,
        )
        copy.start()
        started.append(copy)

    def await_recv(dst, send_sem, recv_sem, device):
        pltpu.make_async_remote_copy(
            src_ref=dst,
            dst_ref=dst,
            send_sem=send_sem,
            recv_sem=recv_sem,
            device_id=device,
            device_id_type=MESH,
        ).wait_recv()

    per_item = chips - 1
    total = ITEMS * per_item

    def piece(index, direction):
        item, at = divmod(index, per_item)
        hop, second = divmod(at, 2)
        half = second if direction == 0 else 1 - second
        return item, hop, half

    def origin(hop, direction, side):
        return lon_at(place - hop if direction == 0 else place + hop, side)

    def ring_step(index):
        got = index - 2
        if 0 <= got < total:
            for direction in range(2):
                item, hop, half = piece(got, direction)
                ref = slot(item, origin(hop + 1, direction, core), half)
                device = right if direction == 0 else left
                await_recv(ref, ring_send.at[direction, got], ring_recv.at[direction, got], device)
                send(ref, ref, sib_send.at[direction, got], sib_recv.at[direction, got], sibling)
        if index < total:
            for direction in range(2):
                item, hop, half = piece(index, direction)
                ref = slot(item, origin(hop, direction, core), half)
                device = right if direction == 0 else left
                send(
                    ref,
                    ref,
                    ring_send.at[direction, index],
                    ring_recv.at[direction, index],
                    device,
                )

    def await_sibling(item):
        ref = slot(item, chip * 2 + 1 - core, 2)
        await_recv(ref, own_send.at[item], own_recv.at[item], sibling)
        for at in range(per_item):
            index = item * per_item + at
            for direction in range(2):
                _, hop, half = piece(index, direction)
                ref = slot(item, origin(hop + 1, direction, 1 - core), half)
                await_recv(
                    ref, sib_send.at[direction, index], sib_recv.at[direction, index], sibling
                )

    tile = 512 if width % 512 == 0 else width

    def project(source, j, write):
        @pl.loop(0, width // tile)
        def _(at):
            start = pl.multiple_of(at * tile, tile)
            acc = None
            for t in range(n_tp):
                term = jnp.dot(
                    source(t),
                    weights[j, t * feat : (t + 1) * feat, pl.ds(start, tile)],
                    preferred_element_type=jnp.float32,
                )
                acc = term if acc is None else acc + term
            write(start, acc)

    def write_normed(dst, row, gain_ref):
        def write(start, acc):
            gain = gain_ref[...]
            for h in range(tile // HEAD):
                dst[row : row + acc.shape[0], pl.ds(start + h * HEAD, HEAD)] = normed(
                    acc[:, h * HEAD : (h + 1) * HEAD], gain
                ).astype(jnp.bfloat16)

        return write

    def write_plain(dst, row):
        def write(start, acc):
            dst[row : row + acc.shape[0], pl.ds(start, tile)] = acc.astype(jnp.bfloat16)

        return write

    def own_tokens(t):
        return tokens[t]

    def style_tokens_of(t):
        return styles[t].reshape(n_lon * style_rows, feat)

    def send_halo(ref, which):
        own = ref.at[pl.ds(count, count), :]
        for side, device in ((0, after), (1, before)):
            send(
                own,
                ref.at[pl.ds(2 * count * side, count), :],
                halo_send.at[which, side],
                halo_recv.at[which, side],
                device,
            )

    def await_halo(ref, which):
        for side, device in ((0, after), (1, before)):
            await_recv(
                ref.at[pl.ds(2 * count * side, count), :],
                halo_send.at[which, side],
                halo_recv.at[which, side],
                device,
            )

    def at_style():
        for k, device in enumerate(peers):
            ref = styles.at[tp, core]
            send(ref, ref, tp_send.at[1, k], tp_recv.at[1, k], device)

    def at_query():
        await_sibling(1)
        for k, device in enumerate(peers):
            ref = tokens.at[lax.rem(tp + n_tp - 1 - k, n_tp)]
            await_recv(ref, tp_send.at[0, k], tp_recv.at[0, k], device)
        project(own_tokens, 0, write_normed(queries, 0, query_gain_ref))

    def at_style_peers():
        for k, device in enumerate(peers):
            ref = styles.at[lax.rem(tp + n_tp - 1 - k, n_tp), core]
            await_recv(ref, tp_send.at[1, k], tp_recv.at[1, k], device)
            send(ref, ref, fwd_send.at[k], fwd_recv.at[k], sibling)

    def at_key():
        await_sibling(2)
        project(own_tokens, 1, write_normed(keys, count, key_gain_ref))
        send_halo(keys, 0)

    def at_style_key():
        await_sibling(0)
        for k in range(n_tp - 1):
            ref = styles.at[lax.rem(tp + n_tp - 1 - k, n_tp), 1 - core]
            await_recv(ref, fwd_send.at[k], fwd_recv.at[k], sibling)
        project(style_tokens_of, 1, write_normed(keys, 3 * count, key_gain_ref))

    def score(first, last):
        bias = jnp.where(flags_ref[0, 0] > 0, 0.0, -1e30).astype(jnp.float32)
        spot = lax.broadcasted_iota(jnp.int32, (1, key_count), 1)
        row = jnp.where(spot < 3 * count, 0.0, bias)

        @pl.loop(first, last)
        def _(h):
            cols = pl.ds(pl.multiple_of(h * HEAD, HEAD), HEAD)
            s = lax.dot_general(
                queries[:, cols], keys[:, cols], NT, preferred_element_type=jnp.float32
            )
            s = s * (1.0 / math.sqrt(HEAD)) + row
            expo = jnp.exp(s - jnp.max(s, axis=-1, keepdims=True))
            inverse = 1.0 / jnp.sum(expo, axis=-1, keepdims=True)
            probs[h] = (expo * inverse).astype(jnp.bfloat16)

    def at_value():
        await_sibling(3)
        project(own_tokens, 2, write_plain(values, count))
        send_halo(values, 1)

    def at_style_value():
        project(style_tokens_of, 2, write_plain(values, 3 * count))

    def attend():
        await_halo(values, 1)

        @pl.loop(0, heads)
        def _(h):
            cols = pl.ds(pl.multiple_of(h * HEAD, HEAD), HEAD)
            attended[:, cols] = jnp.dot(
                probs[h], values[:, cols], preferred_element_type=jnp.float32
            ).astype(jnp.bfloat16)

    pair = max(heads // 4, 1)

    def score_part(quarter):
        if quarter == 0:
            await_halo(keys, 0)
        if quarter * pair < heads:
            score(quarter * pair, quarter * pair + pair)

    hooks = {
        per_item + 2: [at_style],
        2 * per_item + 2: [at_query],
        2 * per_item + 4: [at_style_peers],
        3 * per_item + 2: [at_key],
        3 * per_item + 3: [at_style_key],
        3 * per_item + 4: [functools.partial(score_part, 0)],
        3 * per_item + 5: [functools.partial(score_part, 1)],
        3 * per_item + 6: [functools.partial(score_part, 2)],
        3 * per_item + 7: [functools.partial(score_part, 3)],
        4 * per_item + 2: [at_value],
        4 * per_item + 3: [at_style_value],
        4 * per_item + 5: [attend],
    }

    for index in range(total + 2):
        ring_step(index)
        if index == 0:
            for item in range(ITEMS):
                ref = slot(item, lon, 2)
                send(ref, ref, own_send.at[item], own_recv.at[item], sibling)
            for k, device in enumerate(peers):
                ref = tokens.at[tp]
                send(ref, ref, tp_send.at[0, k], tp_recv.at[0, k], device)
        for hook in hooks.get(index, ()):
            hook()

    await_sibling(4)
    wide = 512 if outw % 512 == 0 else outw

    def columns_of(owner, at):
        rows = pl.ds(pl.multiple_of(owner * outw + at * wide, 16), wide)
        return lax.dot_general(
            attended[...], weights[3, rows, :], NT, preferred_element_type=jnp.float32
        )

    for k, device in enumerate(peers):
        for at in range(outw // wide):
            cols = slice(at * wide, (at + 1) * wide)
            part[k, :, cols] = columns_of(lax.rem(tp + 1 + k, n_tp), at).astype(jnp.bfloat16)
            span = pl.ds(at * wide, wide)
            send(
                part.at[k, :, span],
                arrived.at[k, :, span],
                out_send.at[k, at],
                out_recv.at[k, at],
                device,
            )
    for at in range(outw // wide):
        cols = slice(at * wide, (at + 1) * wide)
        acc = columns_of(tp, at)
        for k, device in enumerate(peers):
            ref = arrived.at[k, :, pl.ds(at * wide, wide)]
            await_recv(ref, out_send.at[k, at], out_recv.at[k, at], device)
            acc = acc + arrived[k, :, cols].astype(jnp.float32)
        mixed_ref[:, cols] = acc.astype(jnp.bfloat16)
    for copy in started:
        copy.wait_send()


def local(n_lon, n_tp, image_tokens, style_tokens, qkv_weight, out_weight, query_gain, key_gain, attend_flags):
    count, feat = image_tokens.shape
    style_rows = style_tokens.shape[0]
    block, width = qkv_weight.shape[1:]
    outw = block * n_lon // n_tp
    key_count = 3 * count + style_rows * n_lon
    chips = n_lon // 2
    pieces = ITEMS * (chips - 1)
    peers = n_tp - 1
    tiles = outw // 512 if outw % 512 == 0 else 1
    bf16 = jnp.bfloat16
    vmem = pl.BlockSpec(memory_space=pltpu.VMEM)
    dma = pltpu.SemaphoreType.DMA
    return pl.pallas_call(
        functools.partial(kernel, n_lon, n_tp),
        out_shape=jax.ShapeDtypeStruct((count, outw), bf16),
        in_specs=[vmem] * 6 + [pl.BlockSpec(memory_space=pltpu.SMEM)],
        out_specs=vmem,
        scratch_shapes=[
            pltpu.VMEM((n_tp, count, feat), bf16),
            pltpu.VMEM((n_tp, 2, chips, style_rows, feat), bf16),
            pltpu.VMEM((4, block * n_lon, width), bf16),
            pltpu.VMEM((count, width), bf16),
            pltpu.VMEM((key_count, width), bf16),
            pltpu.VMEM((key_count, width), bf16),
            pltpu.VMEM((width // HEAD, count, key_count), bf16),
            pltpu.VMEM((count, width), bf16),
            pltpu.VMEM((peers, count, outw), bf16),
            pltpu.VMEM((peers, count, outw), bf16),
            dma((2, pieces)),
            dma((2, pieces)),
            dma((2, pieces)),
            dma((2, pieces)),
            dma((ITEMS,)),
            dma((ITEMS,)),
            dma((2, peers)),
            dma((2, peers)),
            dma((2, 2)),
            dma((2, 2)),
            dma((peers,)),
            dma((peers,)),
            dma((peers, tiles)),
            dma((peers, tiles)),
        ],
        compiler_params=pltpu.CompilerParams(
            collective_id=0, has_side_effects=True, vmem_limit_bytes=60 * 1024 * 1024
        ),
    )(
        image_tokens,
        style_tokens,
        qkv_weight,
        out_weight.T,
        query_gain.reshape(1, HEAD),
        key_gain.reshape(1, HEAD),
        attend_flags,
    )


def solution(mesh):
    in_specs = (
        P("lon", "tp"),
        P("lon", "tp"),
        P(None, "lon", "tp"),
        P("tp", "lon"),
        P(),
        P(),
        P("lon", None),
    )
    inner = functools.partial(local, mesh.shape["lon"], mesh.shape["tp"])
    return jax.shard_map(
        inner, mesh=mesh, in_specs=in_specs, out_specs=P("lon", "tp"), check_vma=False
    )
```

```python
import functools
import math

import jax
import jax.numpy as jnp
from jax import lax
from jax.experimental import pallas as pl
from jax.experimental.pallas import tpu as pltpu
from jax.sharding import PartitionSpec as P

HEAD = 128
ITEMS = 5
WHERE = {1: 1, 2: 0, 3: 2, 4: 3}
MESH = pl.DeviceIdType.MESH
NT = (((1,), (1,)), ((), ()))


def normed(part, gain):
    return part * lax.rsqrt(jnp.mean(part * part, axis=-1, keepdims=True) + 1e-06) * gain


def kernel(
    n_lon,
    n_tp,
    image_ref,
    style_ref,
    qkv_ref,
    out_w_ref,
    query_gain_ref,
    key_gain_ref,
    flags_ref,
    mixed_ref,
    tokens,
    styles,
    weights,
    queries,
    keys,
    values,
    probs,
    attended,
    part,
    arrived,
    ring_send,
    ring_recv,
    sib_send,
    sib_recv,
    own_send,
    own_recv,
    tp_send,
    tp_recv,
    halo_send,
    halo_recv,
    fwd_send,
    fwd_recv,
    out_send,
    out_recv,
):
    count, feat = image_ref.shape
    style_rows = style_ref.shape[0]
    block = qkv_ref.shape[1]
    width = qkv_ref.shape[2]
    heads = width // HEAD
    key_count = keys.shape[0]
    chips = n_lon // 2
    half_ring = chips // 2
    share = chips // n_tp
    lon = lax.axis_index("lon")
    tp = lax.axis_index("tp")
    chip = lon // 2
    core = lon % 2
    odd = chip % 2
    place = (1 - odd) * (chip // 2) + odd * (chips - (chip + 1) // 2)

    def lon_at(position, side):
        position = lax.rem(position + 2 * chips, chips)
        upper = position // half_ring
        there = (1 - upper) * (2 * position) + upper * (2 * chips - 1 - 2 * position)
        return there * 2 + side

    right = {"lon": lon_at(place + 1, core)}
    left = {"lon": lon_at(place - 1, core)}
    sibling = {"lon": chip * 2 + 1 - core}
    after = {"lon": lax.rem(lon + 1, n_lon)}
    before = {"lon": lax.rem(lon + n_lon - 1, n_lon)}
    peers = [{"tp": lax.rem(tp + k, n_tp)} for k in range(1, n_tp)]

    low_w = block // 2 // 16 * 16
    low_s = style_rows // 2 // 16 * 16

    def slot(item, owner, half):
        if item == 0:
            total, low = style_rows, low_s
        else:
            total, low = block, low_w
        start, size = {0: (0, low), 1: (low, total - low), 2: (0, total)}[half]
        if item == 0:
            return styles.at[tp, owner % 2, owner // 2, pl.ds(start, size), :]
        return weights.at[WHERE[item], pl.ds(pl.multiple_of(owner * block, 16) + start, size), :]

    barrier = pltpu.get_barrier_semaphore()
    partners = [right, left, sibling, after, before] + peers
    for partner in partners:
        pl.semaphore_signal(barrier, inc=1, device_id=partner, device_id_type=MESH)

    styles[tp, core, chip] = style_ref[...]
    tokens[tp] = image_ref[...]
    own_rows = pl.ds(pl.multiple_of(lon * block, 16), block)
    for j in range(3):
        weights[j, own_rows, :] = qkv_ref[j]
    weights[3, own_rows, :] = out_w_ref[...]
    pl.semaphore_wait(barrier, len(partners))

    started = []

    def send(src, dst, send_sem, recv_sem, device):
        copy = pltpu.make_async_remote_copy(
            src_ref=src,
            dst_ref=dst,
            send_sem=send_sem,
            recv_sem=recv_sem,
            device_id=device,
            device_id_type=MESH,
        )
        copy.start()
        started.append(copy)

    def await_recv(dst, send_sem, recv_sem, device):
        pltpu.make_async_remote_copy(
            src_ref=dst,
            dst_ref=dst,
            send_sem=send_sem,
            recv_sem=recv_sem,
            device_id=device,
            device_id_type=MESH,
        ).wait_recv()

    per_item = chips - 1
    total = ITEMS * per_item

    def piece(index, direction):
        item, at = divmod(index, per_item)
        hop, second = divmod(at, 2)
        half = second if direction == 0 else 1 - second
        return item, hop, half

    def origin(hop, direction, side):
        return lon_at(place - hop if direction == 0 else place + hop, side)

    def ring_step(index):
        got = index - 2
        if 0 <= got < total:
            for direction in range(2):
                item, hop, half = piece(got, direction)
                ref = slot(item, origin(hop + 1, direction, core), half)
                device = right if direction == 0 else left
                await_recv(ref, ring_send.at[direction, got], ring_recv.at[direction, got], device)
                send(ref, ref, sib_send.at[direction, got], sib_recv.at[direction, got], sibling)
        if index < total:
            for direction in range(2):
                item, hop, half = piece(index, direction)
                ref = slot(item, origin(hop, direction, core), half)
                device = right if direction == 0 else left
                send(
                    ref,
                    ref,
                    ring_send.at[direction, index],
                    ring_recv.at[direction, index],
                    device,
                )

    def await_hop(item, hops):
        if hops == 0:
            ref = slot(item, chip * 2 + 1 - core, 2)
            await_recv(ref, own_send.at[item], own_recv.at[item], sibling)
        for at in range(per_item):
            index = item * per_item + at
            for direction in range(2):
                _, hop, half = piece(index, direction)
                if hop + 1 != hops:
                    continue
                ref = slot(item, origin(hop + 1, direction, 1 - core), half)
                await_recv(
                    ref, sib_send.at[direction, index], sib_recv.at[direction, index], sibling
                )

    def await_sibling(item):
        for hops in range(half_ring + 1):
            await_hop(item, hops)

    tile = 512 if width % 512 == 0 else width
    tiles = width // tile

    def project(source, j, write, first=0, last=tiles):
        @pl.loop(first, last)
        def _(at):
            start = pl.multiple_of(at * tile, tile)
            acc = None
            for t in range(n_tp):
                term = jnp.dot(
                    source(t),
                    weights[j, t * feat : (t + 1) * feat, pl.ds(start, tile)],
                    preferred_element_type=jnp.float32,
                )
                acc = term if acc is None else acc + term
            write(start, acc)

    def write_normed(dst, row, gain_ref):
        def write(start, acc):
            gain = gain_ref[...]
            for h in range(tile // HEAD):
                dst[row : row + acc.shape[0], pl.ds(start + h * HEAD, HEAD)] = normed(
                    acc[:, h * HEAD : (h + 1) * HEAD], gain
                ).astype(jnp.bfloat16)

        return write

    def write_plain(dst, row):
        def write(start, acc):
            dst[row : row + acc.shape[0], pl.ds(start, tile)] = acc.astype(jnp.bfloat16)

        return write

    def own_tokens(t):
        return tokens[t]

    def style_tokens_of(t):
        return styles[t].reshape(n_lon * style_rows, feat)

    def send_halo(ref, which):
        own = ref.at[pl.ds(count, count), :]
        for side, device in ((0, after), (1, before)):
            send(
                own,
                ref.at[pl.ds(2 * count * side, count), :],
                halo_send.at[which, side],
                halo_recv.at[which, side],
                device,
            )

    def await_halo(ref, which):
        for side, device in ((0, after), (1, before)):
            await_recv(
                ref.at[pl.ds(2 * count * side, count), :],
                halo_send.at[which, side],
                halo_recv.at[which, side],
                device,
            )

    def at_style():
        for k, device in enumerate(peers):
            ref = styles.at[tp, core]
            send(ref, ref, tp_send.at[1, k], tp_recv.at[1, k], device)

    def at_query():
        await_sibling(2)
        project(own_tokens, 0, write_normed(queries, 0, query_gain_ref))

    def at_style_peers():
        for k, device in enumerate(peers):
            ref = styles.at[lax.rem(tp + n_tp - 1 - k, n_tp), core]
            await_recv(ref, tp_send.at[1, k], tp_recv.at[1, k], device)
            send(ref, ref, fwd_send.at[k], fwd_recv.at[k], sibling)

    def at_key():
        await_sibling(1)
        for k, device in enumerate(peers):
            ref = tokens.at[lax.rem(tp + n_tp - 1 - k, n_tp)]
            await_recv(ref, tp_send.at[0, k], tp_recv.at[0, k], device)
        project(own_tokens, 1, write_normed(keys, count, key_gain_ref))
        send_halo(keys, 0)

    def at_style_key(at):
        if at == 0:
            await_sibling(0)
            for k in range(n_tp - 1):
                ref = styles.at[lax.rem(tp + n_tp - 1 - k, n_tp), 1 - core]
                await_recv(ref, fwd_send.at[k], fwd_recv.at[k], sibling)
        project(
            style_tokens_of, 1, write_normed(keys, 3 * count, key_gain_ref), at, at + 1
        )

    def score(first, last):
        bias = jnp.where(flags_ref[0, 0] > 0, 0.0, -1e30).astype(jnp.float32)
        spot = lax.broadcasted_iota(jnp.int32, (1, key_count), 1)
        row = jnp.where(spot < 3 * count, 0.0, bias)

        @pl.loop(first, last)
        def _(h):
            cols = pl.ds(pl.multiple_of(h * HEAD, HEAD), HEAD)
            s = lax.dot_general(
                queries[:, cols], keys[:, cols], NT, preferred_element_type=jnp.float32
            )
            s = s * (1.0 / math.sqrt(HEAD)) + row
            expo = jnp.exp(s - jnp.max(s, axis=-1, keepdims=True))
            inverse = 1.0 / jnp.sum(expo, axis=-1, keepdims=True)
            probs[h] = (expo * inverse).astype(jnp.bfloat16)

    def at_value():
        await_sibling(3)
        project(own_tokens, 2, write_plain(values, count))
        send_halo(values, 1)

    def at_style_value(at):
        project(style_tokens_of, 2, write_plain(values, 3 * count), at, at + 1)

    def attend():
        await_halo(values, 1)

        @pl.loop(0, heads)
        def _(h):
            cols = pl.ds(pl.multiple_of(h * HEAD, HEAD), HEAD)
            attended[:, cols] = jnp.dot(
                probs[h], values[:, cols], preferred_element_type=jnp.float32
            ).astype(jnp.bfloat16)

    def score_part(at):
        if at == 0:
            await_halo(keys, 0)
        first, last = heads * at // (per_item - 1), heads * (at + 1) // (per_item - 1)
        if first < last:
            score(first, last)

    def out_block(place_of):
        origin_chip = lon_at(place_of, 0) // 2
        rows = pl.ds(pl.multiple_of(origin_chip * (2 * block), 16), 2 * block)
        part[origin_chip] = lax.dot_general(
            attended[...], weights[3, rows, :], NT, preferred_element_type=jnp.float32
        ).astype(jnp.bfloat16)
        owner = origin_chip // share
        at = lax.rem(origin_chip, share)

        @pl.when(owner != tp)
        def _():
            k = lax.rem(owner - tp + n_tp, n_tp) - 1
            pltpu.make_async_remote_copy(
                src_ref=part.at[origin_chip],
                dst_ref=arrived.at[k, at],
                send_sem=out_send.at[k, at],
                recv_sem=out_recv.at[k, at],
                device_id={"tp": owner},
                device_id_type=MESH,
            ).start()

    def out_hop(hops):
        await_hop(4, hops)
        out_block(place - hops)
        if 0 < hops < half_ring:
            out_block(place + hops)

    hooks = {}

    def plan(index, hook, *args):
        hooks.setdefault(index, []).append(functools.partial(hook, *args))

    plan(per_item + 1, at_style)
    plan(2 * per_item + 1, at_style_peers)
    plan(2 * per_item + 2, at_key)
    for at in range(tiles):
        plan(2 * per_item + 4 + at, at_style_key, at)
        plan(4 * per_item + 3 + at, at_style_value, at)
    plan(3 * per_item + 2, at_query)
    for at in range(per_item - 1):
        plan(3 * per_item + 3 + at, score_part, at)
    plan(4 * per_item + 2, at_value)
    plan(4 * per_item + 3 + tiles, attend)
    for hops in range(half_ring + 1):
        when = max(4 * per_item + 3 + tiles, 4 * per_item + 2 * hops + 2)
        plan(min(when, total + 1), out_hop, hops)

    for index in range(total + 2):
        ring_step(index)
        if index == 0:
            for item in range(ITEMS):
                ref = slot(item, lon, 2)
                send(ref, ref, own_send.at[item], own_recv.at[item], sibling)
            for k, device in enumerate(peers):
                ref = tokens.at[tp]
                send(ref, ref, tp_send.at[0, k], tp_recv.at[0, k], device)
        for hook in hooks.get(index, ()):
            hook()

    for at in range(share):
        acc = part[tp * share + at].astype(jnp.float32)
        for k, device in enumerate(peers):
            ref = arrived.at[k, at]
            await_recv(ref, out_send.at[k, at], out_recv.at[k, at], device)
            acc = acc + arrived[k, at].astype(jnp.float32)
        mixed_ref[at] = acc.astype(jnp.bfloat16)
    for k, device in enumerate(peers):
        owner = lax.rem(tp + 1 + k, n_tp)
        for at in range(share):
            pltpu.make_async_remote_copy(
                src_ref=part.at[owner * share + at],
                dst_ref=arrived.at[k, at],
                send_sem=out_send.at[k, at],
                recv_sem=out_recv.at[k, at],
                device_id=device,
                device_id_type=MESH,
            ).wait_send()
    for copy in started:
        copy.wait_send()


def local(n_lon, n_tp, image_tokens, style_tokens, qkv_weight, out_weight, query_gain, key_gain, attend_flags):
    count, feat = image_tokens.shape
    style_rows = style_tokens.shape[0]
    block, width = qkv_weight.shape[1:]
    outw = block * n_lon // n_tp
    key_count = 3 * count + style_rows * n_lon
    chips = n_lon // 2
    pieces = ITEMS * (chips - 1)
    peers = n_tp - 1
    share = chips // n_tp
    bf16 = jnp.bfloat16
    vmem = pl.BlockSpec(memory_space=pltpu.VMEM)
    dma = pltpu.SemaphoreType.DMA
    mixed = pl.pallas_call(
        functools.partial(kernel, n_lon, n_tp),
        out_shape=jax.ShapeDtypeStruct((share, count, 2 * block), bf16),
        in_specs=[vmem] * 6 + [pl.BlockSpec(memory_space=pltpu.SMEM)],
        out_specs=vmem,
        scratch_shapes=[
            pltpu.VMEM((n_tp, count, feat), bf16),
            pltpu.VMEM((n_tp, 2, chips, style_rows, feat), bf16),
            pltpu.VMEM((4, block * n_lon, width), bf16),
            pltpu.VMEM((count, width), bf16),
            pltpu.VMEM((key_count, width), bf16),
            pltpu.VMEM((key_count, width), bf16),
            pltpu.VMEM((width // HEAD, count, key_count), bf16),
            pltpu.VMEM((count, width), bf16),
            pltpu.VMEM((chips, count, 2 * block), bf16),
            pltpu.VMEM((peers, share, count, 2 * block), bf16),
            dma((2, pieces)),
            dma((2, pieces)),
            dma((2, pieces)),
            dma((2, pieces)),
            dma((ITEMS,)),
            dma((ITEMS,)),
            dma((2, peers)),
            dma((2, peers)),
            dma((2, 2)),
            dma((2, 2)),
            dma((peers,)),
            dma((peers,)),
            dma((peers, share)),
            dma((peers, share)),
        ],
        compiler_params=pltpu.CompilerParams(
            collective_id=0, has_side_effects=True, vmem_limit_bytes=60 * 1024 * 1024
        ),
    )(
        image_tokens,
        style_tokens,
        qkv_weight,
        out_weight.T,
        query_gain.reshape(1, HEAD),
        key_gain.reshape(1, HEAD),
        attend_flags,
    )
    return mixed.transpose(1, 0, 2).reshape(count, outw)


def solution(mesh):
    in_specs = (
        P("lon", "tp"),
        P("lon", "tp"),
        P(None, "lon", "tp"),
        P("tp", "lon"),
        P(),
        P(),
        P("lon", None),
    )
    inner = functools.partial(local, mesh.shape["lon"], mesh.shape["tp"])
    return jax.shard_map(
        inner, mesh=mesh, in_specs=in_specs, out_specs=P("lon", "tp"), check_vma=False
    )
```
